32 devices in a mesh: dp: 8 (over y, x, core), feat: 4 (over z).
Axes of the slice: x: 2, y: 2, z: 4, core: 2. Of those that a mesh axis runs over, the one named last changes fastest.
Arguments:
- dataset: bfloat16 [65536, 4096], P('dp', 'feat'), may hold values from -0.09375 to 0.09375
- targets: float32 [65536], P('dp'), may hold values from 0 to 1
- indices: int32 [16384], P('dp'), may hold values from 0 to 8191
- particles: bfloat16 [384, 4096], P('dp', 'feat'), may hold values from -6 to 6
- spread: int32 [1], replicated, may hold values from 2048 to 8191
Outputs:
- attraction: float32 [384, 4096], P('dp', 'feat')
- repulsion: float32 [384, 4096], P('dp', 'feat')
The draws below stay inside these ranges and needn't reach their ends.
Inputs may be any that keep to these rules, and one draw needn't show every extreme that they name: Entry r of indices names a row within block r // 2048 of the dataset's blocks of 8192 rows.
All inputs are finite; a program needn't handle non-finite values.
Results may differ from the reference program's by a relative error of at most 0.00115.
Values may be sent and summed in bfloat16 or wider, within the bound.
A program may use at most 128 MiB of HBM per device.

```python
import jax
import jax.numpy as jnp
from jax import lax

D = 4096
B_DEV = 2048
DS_DEV = 8192
PARTICLES = 384
BATCH = 16384
DATA = 65536
N_FEAT = 4


def with_ends(values, stream_key, low, high):
    longest = values.shape.index(max(values.shape))
    spots = []
    for shift in (0, 1):
        where = [jax.random.randint(jax.random.fold_in(stream_key, axis), (), 0, length) for axis, length in enumerate(values.shape)]
        where[longest] = (where[longest] + shift) % values.shape[longest]
        spots.append(tuple(where))
    return values.at[spots[0]].set(low).at[spots[1]].set(high)


def block_scale(rng, extent, pieces, smallest, top_value):
    gain, own = 1.0, jax.random.fold_in(rng, 6)
    for dim, parts in pieces:
        steps = jnp.exp(jax.random.uniform(jax.random.fold_in(own, dim), (parts,), jnp.float32, smallest / len(pieces), top_value / len(pieces)))
        gain = gain * jnp.repeat(steps, extent[dim] // parts).reshape([-1 if axis == dim else 1 for axis in range(len(extent))])
    return gain


def noise(own_key, shape, scale, limit, shards=(), kind=jnp.bfloat16):
    array = jax.random.normal(own_key, shape, jnp.float32) * scale
    if len(shards) > 0:
        array = block_scale(own_key, shape, shards, -0.22, 0.18) * array
    return jnp.clip(array, min=-limit, max=limit).astype(kind)


def setup_inputs(seed: int = 0) -> dict:
    key_of = jax.random.split(jax.random.key(seed), 6)
    dataset = noise(key_of[0], (DATA, D), D ** -0.5, 0.09375, ((0, 8), (1, 4)))
    targets = jnp.clip(1.0 * jax.random.uniform(key_of[1], (DATA,), jnp.float32) ** block_scale(key_of[1], (DATA,), ((0, 8),), -0.2, 0.2), 0.0, 1.0)
    indices = with_ends(jax.random.randint(key_of[2], (BATCH,), 0, DS_DEV), jax.random.fold_in(key_of[2], 1), 0, DS_DEV - 1).astype(jnp.int32)
    particles = noise(key_of[3], (PARTICLES, D), 1.0, 6.0, ((0, 8), (1, 4)))
    spread = jax.random.randint(key_of[4], (1,), D // 2, 2 * D).astype(jnp.int32)
    return {"dataset": dataset, "targets": targets, "indices": indices, "particles": particles, "spread": spread}


def reference(dataset, targets, indices, particles, spread):
    row_ids = jnp.arange(BATCH, dtype=jnp.int32)
    rows = (row_ids // B_DEV) * DS_DEV + indices.astype(jnp.int32)
    batch_x = dataset[rows]
    batch_t = targets[rows]
    feat_width = D // N_FEAT
    logits = jnp.zeros((BATCH, PARTICLES), jnp.float32)
    for column in range(N_FEAT):
        low = column * feat_width
        piece_sum = jnp.dot(batch_x[:, low:low + feat_width], particles[:, low:low + feat_width].T, preferred_element_type=jnp.float32)
        rounded = lax.optimization_barrier(piece_sum.astype(jnp.bfloat16))
        logits = logits + rounded.astype(jnp.float32)
    residual = (batch_t[:, None] - jax.nn.sigmoid(logits)).astype(jnp.bfloat16)
    gradient = jnp.dot(residual.T, batch_x, preferred_element_type=jnp.float32)
    theta_f = particles.astype(jnp.float32)
    score = (DS_DEV / B_DEV) * gradient - theta_f
    sq_norms = jnp.sum(theta_f * theta_f, axis=1)
    inner = jnp.dot(particles, particles.T, preferred_element_type=jnp.float32)
    scale_h = spread[0].astype(jnp.float32)
    kernel = jnp.exp(-(sq_norms[:, None] + sq_norms[None, :] - 2.0 * inner) / scale_h)
    attraction = jnp.dot(kernel, score, precision=lax.Precision.HIGHEST) / PARTICLES
    pulled = jnp.dot(kernel, theta_f, precision=lax.Precision.HIGHEST)
    repulsion = (theta_f * jnp.sum(kernel, axis=1)[:, None] - pulled) / PARTICLES
    return attraction, repulsion
```

```python
import functools

import jax
import jax.numpy as jnp
from jax import lax
from jax.experimental import pallas as pl
from jax.experimental.pallas import tpu as pltpu
from jax.sharding import PartitionSpec as P

MESH = pl.DeviceIdType.MESH
CHUNK = 128
LAG = 2
PIECES = 16
HELD = 4


def dot(left, right, contract=((1,), (0,)), precision=None):
    return lax.dot_general(
        left, right, (contract, ((), ())), precision=precision, preferred_element_type=jnp.float32
    )


def gather_orders(bits):
    return [list(range(1, bits)) + [0], list(range(bits - 1, 0, -1)) + [0]]


def scatter_orders(bits):
    return [[0] + list(range(1, bits)), [0] + list(range(bits - 1, 0, -1))]


def patterns(bits):
    found = [0]
    for bit in bits:
        found = found + [value | (1 << bit) for value in found]
    return sorted(found)


def kernel(
    n_dp, n_feat, ratio,
    data_hbm, targets_ref, row_ref, index_ref, own_ref, spread_ref,
    attraction_ref, repulsion_ref,
    data, pieces, x, weights, t_all, inbox, res, grad, inner_out, inner_in, kern, pulled, mixed, landing,
    data_sem, w_send, w_recv, rs_send, rs_recv, ag_send, ag_recv,
    in_send, in_recv, k_send, k_recv, g_send, g_recv,
):
    dp, z = lax.axis_index("dp"), lax.axis_index("feat")
    own, width = own_ref.shape
    half = width // 2
    count = own * n_dp
    side = count // 2
    rows = x.shape[0]
    chunks = rows // CHUNK
    bits = n_dp.bit_length() - 1

    slab = data.shape[0] // PIECES
    loads = [
        pltpu.make_async_copy(
            data_hbm.at[pl.ds(i * slab, slab)], pieces.at[i % HELD], data_sem.at[i]
        )
        for i in range(PIECES)
    ]
    for load in loads[:HELD]:
        load.start()

    barrier = pltpu.get_barrier_semaphore()
    for k in range(1, n_dp):
        pl.semaphore_signal(barrier, inc=1, device_id={"dp": dp ^ k}, device_id_type=MESH)
    for k in range(1, n_feat):
        pl.semaphore_signal(
            barrier, inc=1, device_id={"feat": lax.rem(z + k, n_feat)}, device_id_type=MESH
        )
    pl.semaphore_wait(barrier, n_dp + n_feat - 2)

    def block_rows(j):
        return pl.ds(pl.multiple_of(j * own, own), own)

    weights[block_rows(dp), :] = own_ref[...]
    w_copies = [[], []]
    number = 0
    for h, order in enumerate(gather_orders(bits)):
        for i, bit in enumerate(order):
            done = sum(1 << b for b in order[:i])
            group = []
            for pattern in patterns(order[:i]):
                j = (dp & (n_dp - 1 - done)) | pattern
                place = weights.at[block_rows(j), pl.ds(h * half, half)]
                group.append(pltpu.make_async_remote_copy(
                    src_ref=place, dst_ref=place, send_sem=w_send.at[number], recv_sem=w_recv.at[number],
                    device_id={"dp": dp ^ (1 << bit)}, device_id_type=MESH,
                ))
                number += 1
            w_copies[h].append(group)
    for h in range(2):
        for copy in w_copies[h][0]:
            copy.start()

    index_row = row_ref[...]
    table = targets_ref[...]
    for c in range(chunks):
        part = index_row[:, c * CHUNK:(c + 1) * CHUNK]
        column = lax.broadcasted_iota(jnp.int32, (128, CHUNK), 0)
        hot = jnp.where(column == part % 128, 1.0, 0.0)
        picked = dot(table, hot, precision=lax.Precision.HIGHEST)
        line = lax.broadcasted_iota(jnp.int32, picked.shape, 0)
        t_all[c] = jnp.sum(jnp.where(line == part // 128, picked, 0.0), axis=0, keepdims=True)
    grad[...] = jnp.zeros_like(grad)

    def widen_piece(i):
        loads[i].wait()

        def widen(g, _):
            start = pl.multiple_of(g * 32, 32)
            data[pl.ds(i * slab + start, 32), :] = pieces[i % HELD, pl.ds(start, 32), :].astype(jnp.float32)
            return 0

        lax.fori_loop(0, slab // 32, widen, 0)
        if i + HELD < PIECES:
            loads[i + HELD].start()

    for i in range(bits):
        for piece in range(i * PIECES // bits, (i + 1) * PIECES // bits):
            widen_piece(piece)
        for h in range(2):
            for copy in w_copies[h][i]:
                copy.wait_recv()
            if i + 1 < bits:
                for copy in w_copies[h][i + 1]:
                    copy.start()

    inner_out[pl.ds(0, own), :] = dot(own_ref[...], weights[...], ((1,), (1,)))
    squares = jnp.square(weights[...].astype(jnp.float32))
    inner_out[pl.ds(own, 8), :] = dot(
        jnp.ones((8, width), jnp.float32), squares, ((1,), (1,)), lax.Precision.HIGHEST
    )
    in_copies = [
        pltpu.make_async_remote_copy(
            src_ref=inner_out, dst_ref=inner_in.at[k - 1], send_sem=in_send.at[k - 1],
            recv_sem=in_recv.at[k - 1],
            device_id={"feat": lax.rem(z + k, n_feat)}, device_id_type=MESH,
        )
        for k in range(1, n_feat)
    ]
    for copy in in_copies:
        copy.start()

    def gather(c):
        def group(g, _):
            first = pl.multiple_of(c * CHUNK + g * 16, 16)
            place = lax.broadcasted_iota(jnp.int32, (8, width), 0)
            tiles = []
            for upper in range(2):
                tile = jnp.zeros((8, width), jnp.float32)
                for j in range(8):
                    row = data[pl.ds(index_ref[first + upper * 8 + j], 1), :]
                    tile = jnp.where(place == j, jnp.broadcast_to(row, tile.shape), tile)
                tiles.append(tile)
            x[pl.ds(first, 16), :] = jnp.concatenate(tiles, axis=0).astype(jnp.bfloat16)
            return 0

        lax.fori_loop(0, CHUNK // 16, group, 0)

    def x_chunk(c):
        return x[pl.ds(pl.multiple_of(c * CHUNK, CHUNK), CHUNK), :]

    last = n_feat - 1
    ways = [(z, 1), (last - z, -1)]

    def sum_copy(d, c):
        return pltpu.make_async_remote_copy(
            src_ref=inbox.at[d, c], dst_ref=inbox.at[d, c], send_sem=rs_send.at[d, c],
            recv_sem=rs_recv.at[d, c], device_id={"feat": z + ways[d][1]}, device_id_type=MESH,
        )

    def res_copy(d, c):
        return pltpu.make_async_remote_copy(
            src_ref=res.at[d, c], dst_ref=res.at[d, c], send_sem=ag_send.at[d, c],
            recv_sem=ag_recv.at[d, c], device_id={"feat": z - ways[d][1]}, device_id_type=MESH,
        )

    def slot(s):
        for d, (pos, _) in enumerate(ways):
            c = s - LAG * pos

            @pl.when((c >= 0) & (c < chunks))
            def _():
                part = dot(weights[d * side:(d + 1) * side, :], x_chunk(c), ((1,), (1,)))
                part = part.astype(jnp.bfloat16)

                @pl.when(pos == 0)
                def _():
                    inbox[d, c] = part
                    sum_copy(d, c).start()

                @pl.when((pos > 0) & (pos < last))
                def _():
                    sum_copy(d, c).wait_recv()
                    total = inbox[d, c].astype(jnp.float32) + part.astype(jnp.float32)
                    inbox[d, c] = total.astype(jnp.bfloat16)
                    sum_copy(d, c).start()

                @pl.when(pos == last)
                def _():
                    sum_copy(d, c).wait_recv()
                    total = inbox[d, c].astype(jnp.float32) + part.astype(jnp.float32)
                    res[d, c] = (t_all[c] - jax.nn.sigmoid(total)).astype(jnp.bfloat16)
                    res_copy(d, c).start()

        for d, (pos, _) in enumerate(ways):
            c = s - LAG * (2 * last - pos)

            @pl.when((c >= 0) & (c < chunks) & (pos < last))
            def _():
                res_copy(d, c).wait_recv()

                @pl.when(pos > 0)
                def _():
                    res_copy(d, c).start()

        @pl.when(s + 1 < chunks)
        def _():
            gather(s + 1)

        c = s - LAG * 2 * last

        @pl.when(c >= 0)
        def _():
            for d in range(2):
                grad[d * side:(d + 1) * side, :] += dot(res[d, c], x_chunk(c))

    def run(start, stop):
        def step(s, _):
            slot(s)
            return 0

        lax.fori_loop(start, stop, step, 0)

    gather(0)
    run(0, 2)

    for copy in in_copies:
        copy.wait_recv()
    inner = inner_out[...]
    for k in range(n_feat - 1):
        inner = inner + inner_in[k]
    norms, inner = inner[own:own + 1], inner[:own]
    line = lax.broadcasted_iota(jnp.int32, inner.shape, 0)
    column = lax.broadcasted_iota(jnp.int32, inner.shape, 1)
    own_norms = jnp.sum(jnp.where(column == line + dp * own, inner, 0.0), axis=1, keepdims=True)
    scale = spread_ref[0].astype(jnp.float32)
    own_kernel = jnp.exp(-(own_norms + norms - 2.0 * inner) / scale)
    kern[block_rows(dp), :] = own_kernel
    k_copies = [
        pltpu.make_async_remote_copy(
            src_ref=kern.at[block_rows(dp)], dst_ref=kern.at[block_rows(dp)], send_sem=k_send.at[k - 1],
            recv_sem=k_recv.at[k - 1], device_id={"dp": dp ^ k}, device_id_type=MESH,
        )
        for k in range(1, n_dp)
    ]
    for copy in k_copies:
        copy.start()
    coarse = own_kernel.astype(jnp.bfloat16)
    fine = (own_kernel - coarse.astype(jnp.float32)).astype(jnp.bfloat16)
    pulled[...] = dot(coarse, weights[...]) + dot(fine, weights[...])
    total = jnp.sum(own_kernel, axis=1, keepdims=True)
    repulsion_ref[...] = (own_ref[...].astype(jnp.float32) * total - pulled[...]) / count

    run(2, chunks + LAG * 2 * last)

    for copy in k_copies:
        copy.wait_recv()
    orders = scatter_orders(bits)
    g_copies = [[], []]
    number = 0
    for h, order in enumerate(orders):
        for i, bit in enumerate(order):
            done = sum(1 << b for b in order[:i])
            group = []
            for pattern in patterns(order[i + 1:]):
                kept = (dp & (done | (1 << bit))) | pattern
                sent = kept ^ (1 << bit)
                group.append((kept, number, pltpu.make_async_remote_copy(
                    src_ref=mixed.at[h, sent], dst_ref=landing.at[number], send_sem=g_send.at[number],
                    recv_sem=g_recv.at[number], device_id={"dp": dp ^ (1 << bit)}, device_id_type=MESH,
                )))
                number += 1
            g_copies[h].append(group)

    def mix(j):
        rows_j = kern[block_rows(j), :]
        for h in range(2):
            mixed[h, j] = ratio * dot(
                rows_j, grad[:, h * half:(h + 1) * half], precision=lax.Precision.HIGHEST
            )

    first = [kept for kept, _, _ in g_copies[0][0]]
    for place, kept in enumerate(first):
        mix(kept ^ 1)
        for h in range(2):
            g_copies[h][0][place][2].start()
    for kept in first:
        mix(kept)
    for i in range(bits):
        for h in range(2):
            for kept, place, copy in g_copies[h][i]:
                copy.wait_recv()
                mixed[h, kept] += landing[place]
            if i + 1 < bits:
                for _, _, copy in g_copies[h][i + 1]:
                    copy.start()
    for h in range(2):
        columns = slice(h * half, (h + 1) * half)
        attraction_ref[:, columns] = (mixed[h, dp] - pulled[:, columns]) / count

    for h in range(2):
        for group in w_copies[h]:
            for copy in group:
                copy.wait_send()
        for group in g_copies[h]:
            for _, _, copy in group:
                copy.wait_send()
    for copy in in_copies + k_copies:
        copy.wait_send()

    def drain(c, _):
        for d, (pos, _) in enumerate(ways):
            @pl.when(pos < last)
            def _():
                sum_copy(d, c).wait_send()

            @pl.when(pos > 0)
            def _():
                res_copy(d, c).wait_send()
        return 0

    lax.fori_loop(0, chunks, drain, 0)


def body(n_dp, n_feat, dataset, targets, indices, particles, spread):
    own, width = particles.shape
    count, rows = own * n_dp, indices.shape[0]
    chunks, side = rows // CHUNK, own * n_dp // 2
    vmem = pl.BlockSpec(memory_space=pltpu.VMEM)
    smem = pl.BlockSpec(memory_space=pltpu.SMEM)
    bf16, f32 = jnp.bfloat16, jnp.float32
    dma = pltpu.SemaphoreType.DMA
    steps = 2 * (n_dp - 1)
    return pl.pallas_call(
        functools.partial(kernel, n_dp, n_feat, dataset.shape[0] / rows),
        out_shape=(jax.ShapeDtypeStruct((own, width), f32),) * 2,
        in_specs=[pl.BlockSpec(memory_space=pl.ANY), vmem, vmem, smem, vmem, smem],
        out_specs=(vmem, vmem),
        scratch_shapes=[
            pltpu.VMEM(dataset.shape, f32),
            pltpu.VMEM((HELD, dataset.shape[0] // PIECES, width), bf16),
            pltpu.VMEM((rows, width), bf16),
            pltpu.VMEM((count, width), bf16),
            pltpu.VMEM((chunks, 1, CHUNK), f32),
            pltpu.VMEM((2, chunks, side, CHUNK), bf16),
            pltpu.VMEM((2, chunks, side, CHUNK), bf16),
            pltpu.VMEM((count, width), f32),
            pltpu.VMEM((own + 8, count), f32),
            pltpu.VMEM((n_feat - 1, own + 8, count), f32),
            pltpu.VMEM((count, count), f32),
            pltpu.VMEM((own, width), f32),
            pltpu.VMEM((2, n_dp, own, width // 2), f32),
            pltpu.VMEM((steps, own, width // 2), f32),
            dma((PIECES,)),
            dma((steps,)), dma((steps,)),
            dma((2, chunks)), dma((2, chunks)), dma((2, chunks)), dma((2, chunks)),
            dma((n_feat - 1,)), dma((n_feat - 1,)),
            dma((n_dp - 1,)), dma((n_dp - 1,)),
            dma((steps,)), dma((steps,)),
        ],
        compiler_params=pltpu.CompilerParams(
            collective_id=0, has_side_effects=True, vmem_limit_bytes=60 * 2**20
        ),
        cost_estimate=pl.CostEstimate(
            flops=4 * rows * count * width, bytes_accessed=2 * dataset.size, transcendentals=rows * count
        ),
    )(dataset, targets.reshape(-1, 128), indices.reshape(1, -1), indices, particles, spread)


def solution(mesh):
    return jax.shard_map(
        functools.partial(body, mesh.shape["dp"], mesh.shape["feat"]),
        mesh=mesh,
        in_specs=(P("dp", "feat"), P("dp"), P("dp"), P("dp", "feat"), P()),
        out_specs=(P("dp", "feat"), P("dp", "feat")),
        check_vma=False,
    )
```

```python
import functools

import jax
import jax.numpy as jnp
from jax import lax
from jax.experimental import pallas as pl
from jax.experimental.pallas import tpu as pltpu
from jax.sharding import PartitionSpec as P

MESH = pl.DeviceIdType.MESH
CHUNK = 256
LAG = 1
PIECES = 16
HELD = 4


def dot(left, right, contract=((1,), (0,)), precision=None):
    return lax.dot_general(
        left, right, (contract, ((), ())), precision=precision, preferred_element_type=jnp.float32
    )


def gather_orders(bits):
    return [list(range(1, bits)) + [0], list(range(bits - 1, 0, -1)) + [0]]


def scatter_orders(bits):
    return [[0] + list(range(1, bits)), [0] + list(range(bits - 1, 0, -1))]


def patterns(bits):
    found = [0]
    for bit in bits:
        found = found + [value | (1 << bit) for value in found]
    return sorted(found)


def kernel(
    n_dp, n_feat, ratio,
    data_hbm, targets_ref, row_ref, index_ref, own_ref, spread_ref,
    gained_ref, pulled, scaled_ref,
    data, pieces, x, weights, t_all, inbox, res, grad, inner_out, inner_in, kern, mixed, landing,
    data_sem, w_send, w_recv, rs_send, rs_recv, ag_send, ag_recv,
    in_send, in_recv, k_send, k_recv, g_send, g_recv,
):
    dp, z = lax.axis_index("dp"), lax.axis_index("feat")
    own, width = own_ref.shape
    half = width // 2
    count = own * n_dp
    side = count // 2
    rows = x.shape[0]
    chunks = rows // CHUNK
    bits = n_dp.bit_length() - 1

    slab = data.shape[0] // PIECES
    loads = [
        pltpu.make_async_copy(
            data_hbm.at[pl.ds(i * slab, slab)], pieces.at[i % HELD], data_sem.at[i]
        )
        for i in range(PIECES)
    ]
    for load in loads[:HELD]:
        load.start()

    barrier = pltpu.get_barrier_semaphore()
    for k in range(1, n_dp):
        pl.semaphore_signal(barrier, inc=1, device_id={"dp": dp ^ k}, device_id_type=MESH)
    for k in range(1, n_feat):
        pl.semaphore_signal(
            barrier, inc=1, device_id={"feat": lax.rem(z + k, n_feat)}, device_id_type=MESH
        )
    pl.semaphore_wait(barrier, n_dp + n_feat - 2)

    def block_rows(j):
        return pl.ds(pl.multiple_of(j * own, own), own)

    weights[block_rows(dp), :] = own_ref[...]
    w_copies = [[], []]
    number = 0
    for h, order in enumerate(gather_orders(bits)):
        for i, bit in enumerate(order):
            done = sum(1 << b for b in order[:i])
            group = []
            for pattern in patterns(order[:i]):
                j = (dp & (n_dp - 1 - done)) | pattern
                place = weights.at[block_rows(j), pl.ds(h * half, half)]
                group.append(pltpu.make_async_remote_copy(
                    src_ref=place, dst_ref=place, send_sem=w_send.at[number], recv_sem=w_recv.at[number],
                    device_id={"dp": dp ^ (1 << bit)}, device_id_type=MESH,
                ))
                number += 1
            w_copies[h].append(group)
    for h in range(2):
        for copy in w_copies[h][0]:
            copy.start()

    index_row = row_ref[...]
    table = targets_ref[...]
    for c in range(chunks):
        part = index_row[:, c * CHUNK:(c + 1) * CHUNK]
        column = lax.broadcasted_iota(jnp.int32, (128, CHUNK), 0)
        hot = jnp.where(column == part % 128, 1.0, 0.0)
        picked = dot(table, hot, precision=lax.Precision.HIGHEST)
        line = lax.broadcasted_iota(jnp.int32, picked.shape, 0)
        t_all[c] = jnp.sum(jnp.where(line == part // 128, picked, 0.0), axis=0, keepdims=True)
    grad[...] = jnp.zeros_like(grad)

    def widen_piece(i):
        loads[i].wait()

        def widen(g, _):
            start = pl.multiple_of(g * 32, 32)
            data[pl.ds(i * slab + start, 32), :] = pieces[i % HELD, pl.ds(start, 32), :].astype(jnp.float32)
            return 0

        lax.fori_loop(0, slab // 32, widen, 0)
        if i + HELD < PIECES:
            loads[i + HELD].start()

    for i in range(bits):
        for piece in range(i * PIECES // bits, (i + 1) * PIECES // bits):
            widen_piece(piece)
        for h in range(2):
            for copy in w_copies[h][i]:
                copy.wait_recv()
            if i + 1 < bits:
                for copy in w_copies[h][i + 1]:
                    copy.start()

    def gather(c):
        def group(g, _):
            first = pl.multiple_of(c * CHUNK + g * 16, 16)
            place = lax.broadcasted_iota(jnp.int32, (8, width), 0)
            tiles = []
            for upper in range(2):
                tile = jnp.zeros((8, width), jnp.float32)
                for j in range(8):
                    row = data[pl.ds(index_ref[first + upper * 8 + j], 1), :]
                    tile = jnp.where(place == j, jnp.broadcast_to(row, tile.shape), tile)
                tiles.append(tile)
            x[pl.ds(first, 16), :] = jnp.concatenate(tiles, axis=0).astype(jnp.bfloat16)
            return 0

        lax.fori_loop(0, CHUNK // 16, group, 0)

    def x_chunk(c):
        return x[pl.ds(pl.multiple_of(c * CHUNK, CHUNK), CHUNK), :]

    last = n_feat - 1
    ways = [(z, 1), (last - z, -1)]

    def sum_copy(d, c):
        return pltpu.make_async_remote_copy(
            src_ref=inbox.at[d, c], dst_ref=inbox.at[d, c], send_sem=rs_send.at[d, c],
            recv_sem=rs_recv.at[d, c], device_id={"feat": z + ways[d][1]}, device_id_type=MESH,
        )

    def res_copy(d, c):
        return pltpu.make_async_remote_copy(
            src_ref=res.at[d, c], dst_ref=res.at[d, c], send_sem=ag_send.at[d, c],
            recv_sem=ag_recv.at[d, c], device_id={"feat": z - ways[d][1]}, device_id_type=MESH,
        )

    def slot(s):
        for d, (pos, _) in enumerate(ways):
            c = s - LAG * pos

            @pl.when((c >= 0) & (c < chunks))
            def _():
                part = dot(weights[d * side:(d + 1) * side, :], x_chunk(c), ((1,), (1,)))
                part = part.astype(jnp.bfloat16)

                @pl.when(pos == 0)
                def _():
                    inbox[d, c] = part
                    sum_copy(d, c).start()

                @pl.when((pos > 0) & (pos < last))
                def _():
                    sum_copy(d, c).wait_recv()
                    total = inbox[d, c].astype(jnp.float32) + part.astype(jnp.float32)
                    inbox[d, c] = total.astype(jnp.bfloat16)
                    sum_copy(d, c).start()

                @pl.when(pos == last)
                def _():
                    sum_copy(d, c).wait_recv()
                    total = inbox[d, c].astype(jnp.float32) + part.astype(jnp.float32)
                    res[d, c] = (t_all[c] - jax.nn.sigmoid(total)).astype(jnp.bfloat16)
                    res_copy(d, c).start()

        for d, (pos, _) in enumerate(ways):
            c = s - LAG * (2 * last - pos)

            @pl.when((c >= 0) & (c < chunks) & (pos < last))
            def _():
                res_copy(d, c).wait_recv()

                @pl.when(pos > 0)
                def _():
                    res_copy(d, c).start()

        @pl.when(s + 1 < chunks)
        def _():
            gather(s + 1)

        c = s - LAG * 2 * last

        @pl.when(c >= 0)
        def _():
            for d in range(2):
                grad[d * side:(d + 1) * side, :] += dot(res[d, c], x_chunk(c))

    def run(start, stop):
        def step(s, _):
            slot(s)
            return 0

        lax.fori_loop(start, stop, step, 0)

    gather(0)
    run(0, 1)

    inner_out[pl.ds(0, own), :] = dot(own_ref[...], weights[...], ((1,), (1,)))
    norms = jnp.zeros((8, count), jnp.float32)
    ones = jnp.ones((8, width // 4), jnp.bfloat16)
    for k in range(4):
        squares = jnp.square(weights[:, k * width // 4:(k + 1) * width // 4].astype(jnp.float32))
        upper = squares.astype(jnp.bfloat16)
        lower = (squares - upper.astype(jnp.float32)).astype(jnp.bfloat16)
        norms = norms + dot(ones, upper, ((1,), (1,))) + dot(ones, lower, ((1,), (1,)))
    inner_out[pl.ds(own, 8), :] = norms
    in_copies = [
        pltpu.make_async_remote_copy(
            src_ref=inner_out, dst_ref=inner_in.at[k - 1], send_sem=in_send.at[k - 1],
            recv_sem=in_recv.at[k - 1],
            device_id={"feat": lax.rem(z + k, n_feat)}, device_id_type=MESH,
        )
        for k in range(1, n_feat)
    ]
    for copy in in_copies:
        copy.start()

    run(1, 3)

    for copy in in_copies:
        copy.wait_recv()
    inner = inner_out[...]
    for k in range(n_feat - 1):
        inner = inner + inner_in[k]
    norms, inner = inner[own:own + 1], inner[:own]
    line = lax.broadcasted_iota(jnp.int32, inner.shape, 0)
    column = lax.broadcasted_iota(jnp.int32, inner.shape, 1)
    own_norms = jnp.sum(jnp.where(column == line + dp * own, inner, 0.0), axis=1, keepdims=True)
    scale = spread_ref[0].astype(jnp.float32)
    own_kernel = jnp.exp(-(own_norms + norms - 2.0 * inner) / scale)
    kern_rows = block_rows((dp % 2) * (n_dp // 2) + dp // 2)
    kern[kern_rows, :] = own_kernel
    k_copies = [
        pltpu.make_async_remote_copy(
            src_ref=kern.at[kern_rows], dst_ref=kern.at[kern_rows], send_sem=k_send.at[k - 1],
            recv_sem=k_recv.at[k - 1], device_id={"dp": dp ^ k}, device_id_type=MESH,
        )
        for k in range(1, n_dp)
    ]
    for copy in k_copies:
        copy.start()
    coarse = own_kernel.astype(jnp.bfloat16)
    fine = (own_kernel - coarse.astype(jnp.float32)).astype(jnp.bfloat16)
    pulled[...] = dot(coarse, weights[...]) + dot(fine, weights[...])
    total = jnp.sum(own_kernel, axis=1, keepdims=True)
    scaled_ref[...] = own_ref[...].astype(jnp.float32) * total

    run(3, chunks + LAG * 2 * last)

    for copy in k_copies:
        copy.wait_recv()
    orders = scatter_orders(bits)
    g_copies = [[], []]
    number = 0
    for h, order in enumerate(orders):
        for i, bit in enumerate(order):
            done = sum(1 << b for b in order[:i])
            group = []
            for pattern in patterns(order[i + 1:]):
                kept = (dp & (done | (1 << bit))) | pattern
                sent = kept ^ (1 << bit)
                group.append((kept, number, pltpu.make_async_remote_copy(
                    src_ref=mixed.at[h, sent], dst_ref=landing.at[number], send_sem=g_send.at[number],
                    recv_sem=g_recv.at[number], device_id={"dp": dp ^ (1 << bit)}, device_id_type=MESH,
                )))
                number += 1
            g_copies[h].append(group)

    for h in range(2):
        for group in w_copies[h]:
            for copy in group:
                copy.wait_send()
    for j in range(n_dp):
        piece = slice(j * own, (j + 1) * own)
        upper = grad[piece].astype(jnp.bfloat16)
        weights[piece] = upper
        x[piece] = (grad[piece] - upper.astype(jnp.float32)).astype(jnp.bfloat16)

    def mix(parity):
        taken = min(4, n_dp // 2)
        for q in range(0, n_dp // 2, taken):
            start = pl.multiple_of(parity * side + q * own, own)
            rows_p = ratio * kern[pl.ds(start, taken * own), :]
            coarse = rows_p.astype(jnp.bfloat16)
            fine = (rows_p - coarse.astype(jnp.float32)).astype(jnp.bfloat16)
            for h in range(2):
                columns = slice(h * half, (h + 1) * half)
                sums = dot(coarse, weights[:, columns]) + dot(fine, weights[:, columns])
                sums = sums + dot(coarse, x[:count, columns])
                for k in range(taken):
                    mixed[h, 2 * (q + k) + parity] = sums[k * own:(k + 1) * own]
                if parity is other and q + taken == n_dp // 2:
                    for _, _, copy in g_copies[h][0]:
                        copy.start()

    other = 1 - dp % 2
    mix(other)
    mix(dp % 2)
    for i in range(bits):
        for h in range(2):
            for kept, place, copy in g_copies[h][i]:
                copy.wait_recv()
                mixed[h, kept] += landing[place]
            if i + 1 < bits:
                for _, _, copy in g_copies[h][i + 1]:
                    copy.start()
    for h in range(2):
        columns = slice(h * half, (h + 1) * half)
        gained_ref[:, columns] = mixed[h, dp]

    for h in range(2):
        for group in g_copies[h]:
            for _, _, copy in group:
                copy.wait_send()
    for copy in in_copies + k_copies:
        copy.wait_send()

    def drain(c, _):
        for d, (pos, _) in enumerate(ways):
            @pl.when(pos < last)
            def _():
                sum_copy(d, c).wait_send()

            @pl.when(pos > 0)
            def _():
                res_copy(d, c).wait_send()
        return 0

    lax.fori_loop(0, chunks, drain, 0)


def body(n_dp, n_feat, dataset, targets, indices, particles, spread):
    own, width = particles.shape
    count, rows = own * n_dp, indices.shape[0]
    chunks, side = rows // CHUNK, own * n_dp // 2
    vmem = pl.BlockSpec(memory_space=pltpu.VMEM)
    smem = pl.BlockSpec(memory_space=pltpu.SMEM)
    bf16, f32 = jnp.bfloat16, jnp.float32
    dma = pltpu.SemaphoreType.DMA
    steps = 2 * (n_dp - 1)
    gained, pulled, scaled = pl.pallas_call(
        functools.partial(kernel, n_dp, n_feat, dataset.shape[0] / rows),
        out_shape=(jax.ShapeDtypeStruct((own, width), f32),) * 3,
        in_specs=[pl.BlockSpec(memory_space=pl.ANY), vmem, vmem, smem, vmem, smem],
        out_specs=(vmem, vmem, vmem),
        scratch_shapes=[
            pltpu.VMEM(dataset.shape, f32),
            pltpu.VMEM((HELD, dataset.shape[0] // PIECES, width), bf16),
            pltpu.VMEM((rows, width), bf16),
            pltpu.VMEM((count, width), bf16),
            pltpu.VMEM((chunks, 1, CHUNK), f32),
            pltpu.VMEM((2, chunks, side, CHUNK), bf16),
            pltpu.VMEM((2, chunks, side, CHUNK), bf16),
            pltpu.VMEM((count, width), f32),
            pltpu.VMEM((own + 8, count), f32),
            pltpu.VMEM((n_feat - 1, own + 8, count), f32),
            pltpu.VMEM((count, count), f32),
            pltpu.VMEM((2, n_dp, own, width // 2), f32),
            pltpu.VMEM((steps, own, width // 2), f32),
            dma((PIECES,)),
            dma((steps,)), dma((steps,)),
            dma((2, chunks)), dma((2, chunks)), dma((2, chunks)), dma((2, chunks)),
            dma((n_feat - 1,)), dma((n_feat - 1,)),
            dma((n_dp - 1,)), dma((n_dp - 1,)),
            dma((steps,)), dma((steps,)),
        ],
        compiler_params=pltpu.CompilerParams(
            collective_id=0, has_side_effects=True, vmem_limit_bytes=60 * 2**20
        ),
        cost_estimate=pl.CostEstimate(
            flops=4 * rows * count * width, bytes_accessed=2 * dataset.size, transcendentals=rows * count
        ),
    )(dataset, targets.reshape(-1, 128), indices.reshape(1, -1), indices, particles, spread)
    return (gained - pulled) / count, (scaled - pulled) / count


def solution(mesh):
    return jax.shard_map(
        functools.partial(body, mesh.shape["dp"], mesh.shape["feat"]),
        mesh=mesh,
        in_specs=(P("dp", "feat"), P("dp"), P("dp"), P("dp", "feat"), P()),
        out_specs=(P("dp", "feat"), P("dp", "feat")),
        check_vma=False,
    )
```

```python
import functools

import jax
import jax.numpy as jnp
from jax import lax
from jax.experimental import pallas as pl
from jax.experimental.pallas import tpu as pltpu
from jax.sharding import PartitionSpec as P

MESH = pl.DeviceIdType.MESH
CHUNK = 256
LAG = 1
PIECES = 16
HELD = 4


def dot(left, right, contract=((1,), (0,)), precision=None):
    return lax.dot_general(
        left, right, (contract, ((), ())), precision=precision, preferred_element_type=jnp.float32
    )


def gather_orders(bits):
    return [list(range(1, bits)) + [0], list(range(bits - 1, 0, -1)) + [0]]


def scatter_orders(bits):
    return [[0] + list(range(1, bits)), [0] + list(range(bits - 1, 0, -1))]


def patterns(bits):
    found = [0]
    for bit in bits:
        found = found + [value | (1 << bit) for value in found]
    return sorted(found)


def kernel(
    n_dp, n_feat, ratio,
    data_hbm, targets_ref, row_ref, index_ref, own_ref, spread_ref,
    gained_ref, pulled, scaled_ref,
    data, pieces, picked, x, weights, t_all, inbox, res, grad, inner_out, inner_in, kern, mixed, landing,
    data_sem, w_send, w_recv, rs_send, rs_recv, ag_send, ag_recv,
    in_send, in_recv, k_send, k_recv, g_send, g_recv,
):
    dp, z = lax.axis_index("dp"), lax.axis_index("feat")
    own, width = own_ref.shape
    half = width // 2
    count = own * n_dp
    side = count // 2
    rows = x.shape[0]
    chunks = rows // CHUNK
    bits = n_dp.bit_length() - 1

    slab = data.shape[0] // PIECES
    loads = [
        pltpu.make_async_copy(
            data_hbm.at[pl.ds(i * slab, slab)], pieces.at[i % HELD], data_sem.at[i]
        )
        for i in range(PIECES)
    ]
    for load in loads[:HELD]:
        load.start()

    barrier = pltpu.get_barrier_semaphore()
    for k in range(1, n_dp):
        pl.semaphore_signal(barrier, inc=1, device_id={"dp": dp ^ k}, device_id_type=MESH)
    for k in range(1, n_feat):
        pl.semaphore_signal(
            barrier, inc=1, device_id={"feat": lax.rem(z + k, n_feat)}, device_id_type=MESH
        )
    pl.semaphore_wait(barrier, n_dp + n_feat - 2)

    def block_rows(j):
        return pl.ds(pl.multiple_of(j * own, own), own)

    weights[block_rows(dp), :] = own_ref[...]
    w_copies = [[], []]
    number = 0
    for h, order in enumerate(gather_orders(bits)):
        for i, bit in enumerate(order):
            done = sum(1 << b for b in order[:i])
            group = []
            for pattern in patterns(order[:i]):
                j = (dp & (n_dp - 1 - done)) | pattern
                place = weights.at[block_rows(j), pl.ds(h * half, half)]
                group.append(pltpu.make_async_remote_copy(
                    src_ref=place, dst_ref=place, send_sem=w_send.at[number], recv_sem=w_recv.at[number],
                    device_id={"dp": dp ^ (1 << bit)}, device_id_type=MESH,
                ))
                number += 1
            w_copies[h].append(group)
    for h in range(2):
        for copy in w_copies[h][0]:
            copy.start()

    index_row = row_ref[...]
    table = targets_ref[...]
    for c in range(chunks):
        part = index_row[:, c * CHUNK:(c + 1) * CHUNK]
        column = lax.broadcasted_iota(jnp.int32, (128, CHUNK), 0)
        hot = jnp.where(column == part % 128, 1.0, 0.0)
        chosen = dot(table, hot, precision=lax.Precision.HIGHEST)
        line = lax.broadcasted_iota(jnp.int32, chosen.shape, 0)
        t_all[c] = jnp.sum(jnp.where(line == part // 128, chosen, 0.0), axis=0, keepdims=True)
    grad[...] = jnp.zeros_like(grad)

    def widen_piece(i):
        loads[i].wait()

        def widen(g, _):
            start = pl.multiple_of(g * 32, 32)
            data[pl.ds(i * slab + start, 32), :] = pieces[i % HELD, pl.ds(start, 32), :].astype(jnp.float32)
            return 0

        lax.fori_loop(0, slab // 32, widen, 0)
        if i + HELD < PIECES:
            loads[i + HELD].start()

    for i in range(bits):
        for piece in range(i * PIECES // bits, (i + 1) * PIECES // bits):
            widen_piece(piece)
        for h in range(2):
            for copy in w_copies[h][i]:
                copy.wait_recv()
            if i + 1 < bits:
                for copy in w_copies[h][i + 1]:
                    copy.start()

    def gather(c):
        def group(g, _):
            start = pl.multiple_of(g * 16, 16)
            tile = picked.at[pl.ds(start, 16)]
            for j in range(16):
                tile[j:j + 1, :] = data[pl.ds(index_ref[c * CHUNK + start + j], 1), :]
            return 0

        lax.fori_loop(0, CHUNK // 16, group, 0)
        x[pl.ds(pl.multiple_of(c * CHUNK, CHUNK), CHUNK), :] = picked[...].astype(jnp.bfloat16)
        for d in range(2):
            part = dot(weights[d * side:(d + 1) * side, :], x_chunk(c), ((1,), (1,)))
            res[d, c] = part.astype(jnp.bfloat16)

    def x_chunk(c):
        return x[pl.ds(pl.multiple_of(c * CHUNK, CHUNK), CHUNK), :]

    last = n_feat - 1
    ways = [(z, 1), (last - z, -1)]

    def sum_copy(d, c):
        return pltpu.make_async_remote_copy(
            src_ref=inbox.at[d, c], dst_ref=inbox.at[d, c], send_sem=rs_send.at[d, c],
            recv_sem=rs_recv.at[d, c], device_id={"feat": z + ways[d][1]}, device_id_type=MESH,
        )

    def res_copy(d, c):
        return pltpu.make_async_remote_copy(
            src_ref=res.at[d, c], dst_ref=res.at[d, c], send_sem=ag_send.at[d, c],
            recv_sem=ag_recv.at[d, c], device_id={"feat": z - ways[d][1]}, device_id_type=MESH,
        )

    def slot(s):
        for d, (pos, _) in enumerate(ways):
            c = s - LAG * pos

            @pl.when((c >= 0) & (c < chunks))
            def _():
                part = res[d, c]

                @pl.when(pos == 0)
                def _():
                    inbox[d, c] = part
                    sum_copy(d, c).start()

                @pl.when((pos > 0) & (pos < last))
                def _():
                    sum_copy(d, c).wait_recv()
                    total = inbox[d, c].astype(jnp.float32) + part.astype(jnp.float32)
                    inbox[d, c] = total.astype(jnp.bfloat16)
                    sum_copy(d, c).start()

                @pl.when(pos == last)
                def _():
                    sum_copy(d, c).wait_recv()
                    total = inbox[d, c].astype(jnp.float32) + part.astype(jnp.float32)
                    res[d, c] = (t_all[c] - jax.nn.sigmoid(total)).astype(jnp.bfloat16)
                    res_copy(d, c).start()

        for d, (pos, _) in enumerate(ways):
            c = s - LAG * (2 * last - pos)

            @pl.when((c >= 0) & (c < chunks) & (pos < last))
            def _():
                res_copy(d, c).wait_recv()

                @pl.when(pos > 0)
                def _():
                    res_copy(d, c).start()

        @pl.when(s + 1 < chunks)
        def _():
            gather(s + 1)

        c = s - LAG * 2 * last

        @pl.when(c >= 0)
        def _():
            for d in range(2):
                grad[d * side:(d + 1) * side, :] += dot(res[d, c], x_chunk(c))

    def run(start, stop):
        def step(s, _):
            slot(s)
            return 0

        lax.fori_loop(start, stop, step, 0)

    gather(0)
    run(0, 1)

    inner_out[pl.ds(0, own), :] = dot(own_ref[...], weights[...], ((1,), (1,)))
    norms = jnp.zeros((8, count), jnp.float32)
    ones = jnp.ones((8, width // 4), jnp.bfloat16)
    for k in range(4):
        squares = jnp.square(weights[:, k * width // 4:(k + 1) * width // 4].astype(jnp.float32))
        upper = squares.astype(jnp.bfloat16)
        lower = (squares - upper.astype(jnp.float32)).astype(jnp.bfloat16)
        norms = norms + dot(ones, upper, ((1,), (1,))) + dot(ones, lower, ((1,), (1,)))
    inner_out[pl.ds(own, 8), :] = norms
    in_copies = [
        pltpu.make_async_remote_copy(
            src_ref=inner_out, dst_ref=inner_in.at[k - 1], send_sem=in_send.at[k - 1],
            recv_sem=in_recv.at[k - 1],
            device_id={"feat": lax.rem(z + k, n_feat)}, device_id_type=MESH,
        )
        for k in range(1, n_feat)
    ]
    for copy in in_copies:
        copy.start()

    run(1, 3)

    for copy in in_copies:
        copy.wait_recv()
    inner = inner_out[...]
    for k in range(n_feat - 1):
        inner = inner + inner_in[k]
    norms, inner = inner[own:own + 1], inner[:own]
    line = lax.broadcasted_iota(jnp.int32, inner.shape, 0)
    column = lax.broadcasted_iota(jnp.int32, inner.shape, 1)
    own_norms = jnp.sum(jnp.where(column == line + dp * own, inner, 0.0), axis=1, keepdims=True)
    scale = spread_ref[0].astype(jnp.float32)
    own_kernel = jnp.exp(-(own_norms + norms - 2.0 * inner) / scale)
    kern_rows = block_rows((dp % 2) * (n_dp // 2) + dp // 2)
    kern[kern_rows, :] = own_kernel
    k_copies = [
        pltpu.make_async_remote_copy(
            src_ref=kern.at[kern_rows], dst_ref=kern.at[kern_rows], send_sem=k_send.at[k - 1],
            recv_sem=k_recv.at[k - 1], device_id={"dp": dp ^ k}, device_id_type=MESH,
        )
        for k in range(1, n_dp)
    ]
    for copy in k_copies:
        copy.start()
    coarse = own_kernel.astype(jnp.bfloat16)
    fine = (own_kernel - coarse.astype(jnp.float32)).astype(jnp.bfloat16)
    pulled[...] = dot(coarse, weights[...]) + dot(fine, weights[...])
    total = jnp.sum(own_kernel, axis=1, keepdims=True)
    scaled_ref[...] = own_ref[...].astype(jnp.float32) * total

    run(3, chunks + LAG * 2 * last)

    for copy in k_copies:
        copy.wait_recv()
    orders = scatter_orders(bits)
    g_copies = [[], []]
    number = 0
    for h, order in enumerate(orders):
        for i, bit in enumerate(order):
            done = sum(1 << b for b in order[:i])
            group = []
            for pattern in patterns(order[i + 1:]):
                kept = (dp & (done | (1 << bit))) | pattern
                sent = kept ^ (1 << bit)
                group.append((kept, number, pltpu.make_async_remote_copy(
                    src_ref=mixed.at[h, sent], dst_ref=landing.at[number], send_sem=g_send.at[number],
                    recv_sem=g_recv.at[number], device_id={"dp": dp ^ (1 << bit)}, device_id_type=MESH,
                )))
                number += 1
            g_copies[h].append(group)

    for h in range(2):
        for group in w_copies[h]:
            for copy in group:
                copy.wait_send()
    for j in range(n_dp):
        piece = slice(j * own, (j + 1) * own)
        upper = grad[piece].astype(jnp.bfloat16)
        weights[piece] = upper
        x[piece] = (grad[piece] - upper.astype(jnp.float32)).astype(jnp.bfloat16)

    def mix(parity):
        taken = min(4, n_dp // 2)
        for q in range(0, n_dp // 2, taken):
            start = pl.multiple_of(parity * side + q * own, own)
            rows_p = ratio * kern[pl.ds(start, taken * own), :]
            coarse = rows_p.astype(jnp.bfloat16)
            fine = (rows_p - coarse.astype(jnp.float32)).astype(jnp.bfloat16)
            for h in range(2):
                columns = slice(h * half, (h + 1) * half)
                sums = dot(coarse, weights[:, columns]) + dot(fine, weights[:, columns])
                sums = sums + dot(coarse, x[:count, columns])
                for k in range(taken):
                    mixed[h, 2 * (q + k) + parity] = sums[k * own:(k + 1) * own]
                if parity is other and q + taken == n_dp // 2:
                    for _, _, copy in g_copies[h][0]:
                        copy.start()

    other = 1 - dp % 2
    mix(other)
    mix(dp % 2)
    for i in range(bits):
        for h in range(2):
            for kept, place, copy in g_copies[h][i]:
                copy.wait_recv()
                mixed[h, kept] += landing[place]
            if i + 1 < bits:
                for _, _, copy in g_copies[h][i + 1]:
                    copy.start()
    for h in range(2):
        columns = slice(h * half, (h + 1) * half)
        gained_ref[:, columns] = mixed[h, dp]

    for h in range(2):
        for group in g_copies[h]:
            for _, _, copy in group:
                copy.wait_send()
    for copy in in_copies + k_copies:
        copy.wait_send()

    def drain(c, _):
        for d, (pos, _) in enumerate(ways):
            @pl.when(pos < last)
            def _():
                sum_copy(d, c).wait_send()

            @pl.when(pos > 0)
            def _():
                res_copy(d, c).wait_send()
        return 0

    lax.fori_loop(0, chunks, drain, 0)


def body(n_dp, n_feat, dataset, targets, indices, particles, spread):
    own, width = particles.shape
    count, rows = own * n_dp, indices.shape[0]
    chunks, side = rows // CHUNK, own * n_dp // 2
    vmem = pl.BlockSpec(memory_space=pltpu.VMEM)
    smem = pl.BlockSpec(memory_space=pltpu.SMEM)
    bf16, f32 = jnp.bfloat16, jnp.float32
    dma = pltpu.SemaphoreType.DMA
    steps = 2 * (n_dp - 1)
    gained, pulled, scaled = pl.pallas_call(
        functools.partial(kernel, n_dp, n_feat, dataset.shape[0] / rows),
        out_shape=(jax.ShapeDtypeStruct((own, width), f32),) * 3,
        in_specs=[pl.BlockSpec(memory_space=pl.ANY), vmem, vmem, smem, vmem, smem],
        out_specs=(vmem, vmem, vmem),
        scratch_shapes=[
            pltpu.VMEM(dataset.shape, f32),
            pltpu.VMEM((HELD, dataset.shape[0] // PIECES, width), bf16),
            pltpu.VMEM((CHUNK, width), f32),
            pltpu.VMEM((rows, width), bf16),
            pltpu.VMEM((count, width), bf16),
            pltpu.VMEM((chunks, 1, CHUNK), f32),
            pltpu.VMEM((2, chunks, side, CHUNK), bf16),
            pltpu.VMEM((2, chunks, side, CHUNK), bf16),
            pltpu.VMEM((count, width), f32),
            pltpu.VMEM((own + 8, count), f32),
            pltpu.VMEM((n_feat - 1, own + 8, count), f32),
            pltpu.VMEM((count, count), f32),
            pltpu.VMEM((2, n_dp, own, width // 2), f32),
            pltpu.VMEM((steps, own, width // 2), f32),
            dma((PIECES,)),
            dma((steps,)), dma((steps,)),
            dma((2, chunks)), dma((2, chunks)), dma((2, chunks)), dma((2, chunks)),
            dma((n_feat - 1,)), dma((n_feat - 1,)),
            dma((n_dp - 1,)), dma((n_dp - 1,)),
            dma((steps,)), dma((steps,)),
        ],
        compiler_params=pltpu.CompilerParams(
            collective_id=0, has_side_effects=True, vmem_limit_bytes=60 * 2**20
        ),
        cost_estimate=pl.CostEstimate(
            flops=4 * rows * count * width, bytes_accessed=2 * dataset.size, transcendentals=rows * count
        ),
    )(dataset, targets.reshape(-1, 128), indices.reshape(1, -1), indices, particles, spread)
    return (gained - pulled) / count, (scaled - pulled) / count


def solution(mesh):
    return jax.shard_map(
        functools.partial(body, mesh.shape["dp"], mesh.shape["feat"]),
        mesh=mesh,
        in_specs=(P("dp", "feat"), P("dp"), P("dp"), P("dp", "feat"), P()),
        out_specs=(P("dp", "feat"), P("dp", "feat")),
        check_vma=False,
    )
```
